512 devices in a mesh: row: 64 (over z, y), col: 8 (over x, core).
Axes of the slice: x: 4, y: 4, z: 16, core: 2. Of those that a mesh axis runs over, the one named last changes fastest.
Arguments:
- activations: bfloat16 [131072, 8192], P('row', 'col'), may hold values from -640 to 640
- start_basis: bfloat16 [8192, 256], P('col'), may hold values from -0.0625 to 0.0625
Outputs:
- basis: bfloat16 [131072, 256], P('row', 'col')
- projected: float32 [256, 8192], P('row', 'col')
The draws below stay inside these ranges and needn't reach their ends.
All inputs are finite; a program needn't handle non-finite values.
Results may differ from the reference program's by a relative error of at most 0.023.
Values may be sent and summed in bfloat16 or wider, within the bound.
No kernel may reach another device: no remote copies, remote signals or barrier semaphores. Data moves between devices by JAX's collectives and lax.ppermute only.
A program may use at most 64 MiB of HBM per device.

```python
import math
import jax
import jax.numpy as jnp
from jax import lax

D = 8192
K = 256
ROWS_DEV = 2048
TOKENS = 131072


def draw_activations(key, part):
    key = jax.random.fold_in(key, 1)
    key_base, key_rows, key_cols, key_block, key_heavy = jax.random.split(key, 5)
    block_count = TOKENS // ROWS_DEV
    base = jax.random.truncated_normal(key_base, -4.0, 4.0, (TOKENS, D), jnp.float32)
    row_scale = jnp.exp(jax.random.uniform(key_rows, (TOKENS, 1), jnp.float32, 0.0, math.log(10.0)))
    col_scale = jnp.exp(jax.random.uniform(key_cols, (1, D), jnp.float32, math.log(0.1), 0.0))
    block_level = jax.random.uniform(key_block, (block_count,), jnp.float32, 0.0, 1.0)
    heavy_block = jax.random.randint(key_heavy, (), 0, block_count)
    block_level = jnp.where(jnp.arange(block_count) == heavy_block, 1.0, block_level)
    block_scale = jnp.exp(block_level * block_level * math.log(16.0))
    token_scale = jnp.repeat(block_scale, ROWS_DEV)[:, None]
    return (base * row_scale * col_scale * token_scale).astype(jnp.bfloat16)


def block_levels(key, dims, cuts, least, top_value):
    factor_of = 1.0
    for axis_at, blocks in cuts:
        heights = jax.random.uniform(jax.random.fold_in(jax.random.fold_in(key, 6), axis_at), (blocks,), jnp.float32, least / len(cuts), top_value / len(cuts))
        factor_of = factor_of * jnp.repeat(jnp.exp(heights), dims[axis_at] // blocks).reshape((-1,) + (1,) * (len(dims) - 1 - axis_at))
    return factor_of


def scatter_about(key, dims, scale, bound, cuts=(), kind=jnp.bfloat16):
    level = block_levels(key, dims, cuts, -0.22, 0.18) if cuts else 1.0
    array = jax.random.normal(key, dims, jnp.float32) * scale * level
    return jnp.minimum(jnp.maximum(array, -bound), bound).astype(kind)


def setup_inputs(seed: int = 0) -> dict:
    keys = jax.random.split(jax.random.key(seed), 3)
    return {
        "activations": draw_activations(jax.random.fold_in(keys[2], 71), 0),
        "start_basis": scatter_about(keys[1], (D, K), D ** -0.5, 0.0625, ((0, 8),)),
    }


def reference(activations, start_basis):
    sketch = jnp.dot(activations.astype(jnp.float32), start_basis.astype(jnp.float32), preferred_element_type=jnp.float32)
    gram = lax.dot_general(sketch.astype(jnp.float32), sketch.astype(jnp.float32), (((0,), (0,)), ((), ())), precision=lax.Precision.HIGHEST, preferred_element_type=jnp.float32)
    lower_factor = jnp.linalg.cholesky(gram)
    solved = lax.linalg.triangular_solve(lower_factor, sketch, left_side=False, lower=True, transpose_a=True)
    root_tokens = math.sqrt(TOKENS)
    basis = (solved * root_tokens).astype(jnp.bfloat16)
    projected = lax.dot_general(basis.astype(jnp.float32), activations.astype(jnp.float32), (((0,), (0,)), ((), ())), preferred_element_type=jnp.float32) / root_tokens
    return (basis, projected)
```

```python
import math

import jax
import jax.numpy as jnp
from jax import lax
from jax.sharding import PartitionSpec as P

Y = 4


def groups(rows, cols):
    depth = rows // Y
    plane = [[(z * Y + y) * cols + c for y in range(Y) for c in range(cols)] for z in range(depth)]
    along_z = [[z * Y + y for z in range(depth)] for y in range(Y)]
    return plane, along_z


def exchange(blocks, axis, members=None):
    return lax.all_to_all(blocks, axis, 0, 0, axis_index_groups=members)


def share(block, count, axis, members=None):
    return exchange(jnp.broadcast_to(block[None], (count,) + block.shape), axis, members)


def local(activations, start_basis):
    rows, cols = lax.axis_size("row"), lax.axis_size("col")
    rows_dev, rank = activations.shape[0], start_basis.shape[1]
    root_tokens = math.sqrt(rows_dev * rows)
    plane, along_z = groups(rows, cols)
    plane_size, depth = Y * cols, rows // Y

    partial = jnp.dot(activations, start_basis, preferred_element_type=jnp.float32)
    partial = partial.astype(jnp.bfloat16).reshape(cols, rows_dev // cols, rank)
    own = jnp.sum(exchange(partial, "col").astype(jnp.float32), 0).astype(jnp.bfloat16)
    sketch = share(own, cols, "col").reshape(rows_dev, rank)

    gram = lax.dot_general(own, own, (((0,), (0,)), ((), ())), preferred_element_type=jnp.float32)
    gram = gram.reshape(plane_size, rank // plane_size, rank)
    gram = jnp.sum(exchange(gram, ("row", "col"), plane), 0)
    gram = jnp.sum(share(gram, depth, "row", along_z), 0)
    gram = share(gram, plane_size, ("row", "col"), plane).reshape(rank, rank)

    lower = lax.linalg.cholesky(gram, symmetrize_input=False)
    inverse = lax.linalg.triangular_solve(
        lower, jnp.eye(rank, dtype=jnp.float32), left_side=True, lower=True
    )
    inverse = inverse * root_tokens
    high = inverse.astype(jnp.bfloat16)
    low = (inverse - high.astype(jnp.float32)).astype(jnp.bfloat16)
    by_rows = (((1,), (1,)), ((), ()))
    basis = lax.dot_general(sketch, high, by_rows, preferred_element_type=jnp.float32)
    basis = basis + lax.dot_general(sketch, low, by_rows, preferred_element_type=jnp.float32)
    basis = basis.astype(jnp.bfloat16)

    projected = lax.dot_general(
        basis, activations, (((0,), (0,)), ((), ())), preferred_element_type=jnp.float32
    )
    projected = projected.astype(jnp.bfloat16).reshape(rows, rank // rows, -1)
    projected = jnp.sum(exchange(projected, "row").astype(jnp.float32), 0) / root_tokens

    width = rank // cols
    basis = lax.dynamic_slice_in_dim(basis, lax.axis_index("col") * width, width, 1)
    return (basis, projected)


def solution(mesh):
    return jax.shard_map(
        local,
        mesh=mesh,
        in_specs=(P("row", "col"), P("col", None)),
        out_specs=(P("row", "col"), P("row", "col")),
        check_vma=False,
    )
```

```python
import functools
import math

import jax
import jax.numpy as jnp
from jax import lax
from jax.experimental import pallas as pl
from jax.experimental.pallas import tpu as pltpu
from jax.sharding import PartitionSpec as P

Y = 4
PANEL, SUB, LANES = 32, 8, 128


def groups(rows, cols):
    depth = rows // Y
    plane = [[(z * Y + y) * cols + c for y in range(Y) for c in range(cols)] for z in range(depth)]
    along_z = [[z * Y + y for z in range(depth)] for y in range(Y)]
    along_y = [[z * Y + y for y in range(Y)] for z in range(depth)]
    return plane, along_y, along_z


def exchange(blocks, axis, members=None):
    return lax.all_to_all(blocks, axis, 0, 0, axis_index_groups=members)


def share(block, count, axis, members=None):
    return exchange(jnp.broadcast_to(block[None], (count,) + block.shape), axis, members)


def factor_kernel(gram_ref, high_ref, low_ref, work, *, scale):
    size = gram_ref.shape[0]
    count, spans = PANEL // SUB, size // LANES
    f32 = jnp.float32
    sub = lax.broadcasted_iota(jnp.int32, (SUB, LANES), 0)
    lanes = lax.broadcasted_iota(jnp.int32, (SUB, LANES), 1)
    work[...] = gram_ref[...]

    def spread(row):
        return jnp.broadcast_to(row, (SUB, LANES))

    def wide(columns):
        return jnp.concatenate([jnp.concatenate([c] * spans, axis=1) for c in columns], axis=0)

    def panel(index, carry):
        start = pl.multiple_of(index * PANEL, PANEL)
        rows = work[pl.ds(start, PANEL), :]
        diagonal = pltpu.roll(rows, (size - start) % size, 1)
        tiles = []
        for g in range(count):
            line = []
            for t in range(spans):
                at = lanes + LANES * t - start
                inside = (at >= 0) & (at < PANEL)
                unit = (at == sub + SUB * g).astype(f32)
                block = rows[SUB * g : SUB * (g + 1), LANES * t : LANES * (t + 1)]
                line.append(jnp.where(inside, unit, block))
            tiles.append(line + [diagonal[SUB * g : SUB * (g + 1), :LANES]])
        inverses, pivots = [], []
        for g in range(count):
            left = range(g, count)
            columns = [
                {h: spread(tiles[h][spans][:, SUB * g + j : SUB * g + j + 1]) for h in left}
                for j in range(SUB)
            ]
            inverse_of, pivot_of = jnp.ones((SUB, LANES), f32), jnp.ones((SUB, LANES), f32)
            for j in range(SUB):
                pivot = spread(columns[j][g][j : j + 1])
                inverse = 1.0 / pivot
                factors = {h: columns[j][h] * inverse for h in left}
                factors[g] = jnp.where(sub > j, factors[g], 0.0)
                for k in range(j + 1, SUB):
                    row = spread(columns[k][g][j : j + 1])
                    for h in left:
                        columns[k][h] = columns[k][h] - factors[h] * row
                for t in range(spans + (g < count - 1)):
                    row = spread(tiles[g][t][j : j + 1])
                    for h in left:
                        tiles[h][t] = tiles[h][t] - factors[h] * row
                inverse_of = jnp.where(sub == j, inverse, inverse_of)
                pivot_of = jnp.where(sub == j, pivot, pivot_of)
            inverses.append(inverse_of)
            pivots.append(pivot_of)
        done = jnp.concatenate([jnp.concatenate(line[:spans], axis=1) for line in tiles], axis=0)
        lane = lax.broadcasted_iota(jnp.int32, (PANEL, size), 1)
        result = done * wide([lax.rsqrt(p) * scale for p in pivots])
        result = jnp.where(lane < start + PANEL, result, 0.0)
        high = result.astype(jnp.bfloat16)
        high_ref[pl.ds(start, PANEL), :] = high
        low_ref[pl.ds(start, PANEL), :] = (result - high.astype(f32)).astype(jnp.bfloat16)
        factors = jnp.where(lane >= start + PANEL, done * wide(inverses), 0.0)
        update = lax.dot_general(
            factors,
            done,
            (((0,), (0,)), ((), ())),
            precision=lax.Precision.HIGHEST,
            preferred_element_type=f32,
        )
        at = lax.broadcasted_iota(jnp.int32, (size, size), 1) - start
        work[...] = jnp.where((at >= 0) & (at < PANEL), 0.0, work[...]) - update
        return carry

    lax.fori_loop(0, size // PANEL, panel, 0)


def inverse_factor(gram, scale):
    pair = jax.ShapeDtypeStruct(gram.shape, jnp.bfloat16)
    return pl.pallas_call(
        functools.partial(factor_kernel, scale=scale),
        out_shape=[pair, pair],
        in_specs=[pl.BlockSpec(memory_space=pltpu.VMEM)],
        out_specs=[pl.BlockSpec(memory_space=pltpu.VMEM)] * 2,
        scratch_shapes=[pltpu.VMEM(gram.shape, jnp.float32)],
        name="inverse_factor",
    )(gram)


def apply_pair(sketch, high, low):
    by_rows = (((1,), (1,)), ((), ()))
    out = lax.dot_general(sketch, high, by_rows, preferred_element_type=jnp.float32)
    out = out + lax.dot_general(sketch, low, by_rows, preferred_element_type=jnp.float32)
    return out.astype(jnp.bfloat16)


def local(activations, start_basis):
    rows, cols = lax.axis_size("row"), lax.axis_size("col")
    rows_dev, rank = activations.shape[0], start_basis.shape[1]
    root_tokens = math.sqrt(rows_dev * rows)
    plane, along_y, along_z = groups(rows, cols)
    plane_size, depth = Y * cols, rows // Y

    partial = jnp.dot(activations, start_basis, preferred_element_type=jnp.float32)
    partial = partial.astype(jnp.bfloat16).reshape(cols, rows_dev // cols, rank)
    own = jnp.sum(exchange(partial, "col").astype(jnp.float32), 0).astype(jnp.bfloat16)
    sketch = share(own, cols, "col").reshape(rows_dev, rank)

    gram = lax.dot_general(own, own, (((0,), (0,)), ((), ())), preferred_element_type=jnp.float32)
    gram = gram.reshape(plane_size, rank // plane_size, rank)
    gram = jnp.sum(exchange(gram, ("row", "col"), plane), 0)
    gram = jnp.sum(share(gram, depth, "row", along_z), 0)
    gram = share(gram, plane_size, ("row", "col"), plane).reshape(rank, rank)

    high, low = inverse_factor(gram, root_tokens)

    def by_y(pair):
        pair = pair.reshape(depth, Y, rank // rows, rank)
        return jnp.swapaxes(pair, 0, 1).reshape(rank, rank)

    turned = apply_pair(sketch, by_y(high), by_y(low))
    projected = lax.dot_general(
        turned, activations, (((0,), (0,)), ((), ())), preferred_element_type=jnp.float32
    )
    projected = projected.astype(jnp.bfloat16).reshape(Y, rank // Y, -1)
    projected = jnp.sum(exchange(projected, "row", along_y).astype(jnp.float32), 0)
    projected = projected.astype(jnp.bfloat16).reshape(depth, rank // rows, -1)
    projected = exchange(projected, "row", along_z).astype(jnp.float32)
    projected = jnp.sum(projected, 0) / root_tokens

    width = rank // cols
    first = lax.axis_index("col") * width
    mine = [lax.dynamic_slice_in_dim(part, first, width, 0) for part in (high, low)]
    return (apply_pair(sketch, *mine), projected)


def solution(mesh):
    return jax.shard_map(
        local,
        mesh=mesh,
        in_specs=(P("row", "col"), P("col", None)),
        out_specs=(P("row", "col"), P("row", "col")),
        check_vma=False,
    )
```

```python
import functools
import math

import jax
import jax.numpy as jnp
from jax import lax
from jax.experimental import pallas as pl
from jax.experimental.pallas import tpu as pltpu
from jax.sharding import PartitionSpec as P

Y = 4
PANEL, SUB, LANES = 64, 8, 128


def groups(rows, cols):
    depth = rows // Y
    plane = [[(z * Y + y) * cols + c for y in range(Y) for c in range(cols)] for z in range(depth)]
    along_z = [[z * Y + y for z in range(depth)] for y in range(Y)]
    along_y = [[z * Y + y for y in range(Y)] for z in range(depth)]
    return plane, along_y, along_z


def exchange(blocks, axis, members=None):
    return lax.all_to_all(blocks, axis, 0, 0, axis_index_groups=members)


def share(block, count, axis, members=None):
    return exchange(jnp.broadcast_to(block[None], (count,) + block.shape), axis, members)


def factor_kernel(gram_ref, high_ref, low_ref, work, *, scale):
    size = gram_ref.shape[0]
    count, spans = PANEL // SUB, size // LANES
    f32 = jnp.float32
    sub = lax.broadcasted_iota(jnp.int32, (SUB, LANES), 0)
    lanes = lax.broadcasted_iota(jnp.int32, (SUB, LANES), 1)
    work[...] = gram_ref[...]

    def spread(row):
        return jnp.broadcast_to(row, (SUB, LANES))

    def wide(columns):
        return jnp.concatenate([jnp.concatenate([c] * spans, axis=1) for c in columns], axis=0)

    def panel(index, carry):
        start = pl.multiple_of(index * PANEL, PANEL)
        rows = work[pl.ds(start, PANEL), :]
        diagonal = pltpu.roll(rows, (size - start) % size, 1)
        tiles = []
        for g in range(count):
            line = []
            for t in range(spans):
                at = lanes + LANES * t - start
                inside = (at >= 0) & (at < PANEL)
                unit = (at == sub + SUB * g).astype(f32)
                block = rows[SUB * g : SUB * (g + 1), LANES * t : LANES * (t + 1)]
                line.append(jnp.where(inside, unit, block))
            tiles.append(line + [diagonal[SUB * g : SUB * (g + 1), :LANES]])
        inverses, pivots = [], []
        for g in range(count):
            left = range(g, count)
            columns = [
                {h: spread(tiles[h][spans][:, SUB * g + j : SUB * g + j + 1]) for h in left}
                for j in range(SUB)
            ]
            inverse_of, pivot_of = jnp.ones((SUB, LANES), f32), jnp.ones((SUB, LANES), f32)
            for j in range(SUB):
                pivot = spread(columns[j][g][j : j + 1])
                inverse = 1.0 / pivot
                factors = {h: columns[j][h] * inverse for h in left}
                factors[g] = jnp.where(sub > j, factors[g], 0.0)
                for k in range(j + 1, SUB):
                    row = spread(columns[k][g][j : j + 1])
                    for h in left:
                        columns[k][h] = columns[k][h] - factors[h] * row
                for t in range(spans + (g < count - 1)):
                    row = spread(tiles[g][t][j : j + 1])
                    for h in left:
                        tiles[h][t] = tiles[h][t] - factors[h] * row
                inverse_of = jnp.where(sub == j, inverse, inverse_of)
                pivot_of = jnp.where(sub == j, pivot, pivot_of)
            inverses.append(inverse_of)
            pivots.append(pivot_of)
        done = jnp.concatenate([jnp.concatenate(line[:spans], axis=1) for line in tiles], axis=0)
        lane = lax.broadcasted_iota(jnp.int32, (PANEL, size), 1)
        result = done * wide([lax.rsqrt(p) * scale for p in pivots])
        result = jnp.where(lane < start + PANEL, result, 0.0)
        high = result.astype(jnp.bfloat16)
        high_ref[pl.ds(start, PANEL), :] = high
        low_ref[pl.ds(start, PANEL), :] = (result - high.astype(f32)).astype(jnp.bfloat16)
        factors = jnp.where(lane >= start + PANEL, done * wide(inverses), 0.0)
        update = lax.dot_general(
            factors,
            done,
            (((0,), (0,)), ((), ())),
            precision=lax.Precision.HIGHEST,
            preferred_element_type=f32,
        )
        at = lax.broadcasted_iota(jnp.int32, (size, size), 1) - start
        work[...] = jnp.where((at >= 0) & (at < PANEL), 0.0, work[...]) - update
        return carry

    lax.fori_loop(0, size // PANEL, panel, 0)


def inverse_factor(gram, scale):
    pair = jax.ShapeDtypeStruct(gram.shape, jnp.bfloat16)
    return pl.pallas_call(
        functools.partial(factor_kernel, scale=scale),
        out_shape=[pair, pair],
        in_specs=[pl.BlockSpec(memory_space=pltpu.VMEM)],
        out_specs=[pl.BlockSpec(memory_space=pltpu.VMEM)] * 2,
        scratch_shapes=[pltpu.VMEM(gram.shape, jnp.float32)],
        name="inverse_factor",
    )(gram)


def project_kernel(sketch_ref, high_ref, low_ref, activations_ref, out_ref, *, depth, lines):
    rank = high_ref.shape[0]
    f32, bf16 = jnp.float32, jnp.bfloat16
    to = lax.broadcasted_iota(jnp.int32, (rank, rank), 0)
    source = lax.broadcasted_iota(jnp.int32, (rank, rank), 1)
    y, z, line = to // (depth * lines), to // lines % depth, to % lines
    turn = (source == (z * Y + y) * lines + line).astype(bf16)
    by_rows = (((1,), (1,)), ((), ()))
    basis = jnp.zeros((rank, sketch_ref.shape[0]), f32)
    for part in (high_ref, low_ref):
        turned = jnp.dot(turn, part[...], preferred_element_type=f32).astype(bf16)
        basis += lax.dot_general(turned, sketch_ref[...], by_rows, preferred_element_type=f32)
    basis = basis.astype(bf16)
    out_ref[...] = jnp.dot(basis, activations_ref[...], preferred_element_type=f32).astype(bf16)


def project(sketch, high, low, activations, depth, lines):
    return pl.pallas_call(
        functools.partial(project_kernel, depth=depth, lines=lines),
        out_shape=jax.ShapeDtypeStruct((high.shape[0], activations.shape[1]), jnp.bfloat16),
        in_specs=[pl.BlockSpec(memory_space=pltpu.VMEM)] * 4,
        out_specs=pl.BlockSpec(memory_space=pltpu.VMEM),
        compiler_params=pltpu.CompilerParams(vmem_limit_bytes=32 * 2**20),
        name="project",
    )(sketch, high, low, activations)


def apply_pair(sketch, high, low):
    by_rows = (((1,), (1,)), ((), ()))
    out = lax.dot_general(sketch, high, by_rows, preferred_element_type=jnp.float32)
    out = out + lax.dot_general(sketch, low, by_rows, preferred_element_type=jnp.float32)
    return out.astype(jnp.bfloat16)


def local(activations, start_basis):
    rows, cols = lax.axis_size("row"), lax.axis_size("col")
    rows_dev, rank = activations.shape[0], start_basis.shape[1]
    root_tokens = math.sqrt(rows_dev * rows)
    plane, along_y, along_z = groups(rows, cols)
    plane_size, depth = Y * cols, rows // Y

    partial = jnp.dot(activations, start_basis, preferred_element_type=jnp.float32)
    partial = partial.astype(jnp.bfloat16).reshape(cols, rows_dev // cols, rank)
    own = jnp.sum(exchange(partial, "col").astype(jnp.float32), 0).astype(jnp.bfloat16)
    sketch = share(own, cols, "col").reshape(rows_dev, rank)

    gram = lax.dot_general(own, own, (((0,), (0,)), ((), ())), preferred_element_type=jnp.float32)
    gram = gram.reshape(plane_size, rank // plane_size, rank)
    gram = jnp.sum(exchange(gram, ("row", "col"), plane), 0)
    gram = jnp.sum(share(gram, depth, "row", along_z), 0)
    gram = share(gram, plane_size, ("row", "col"), plane).reshape(rank, rank)

    high, low = inverse_factor(gram, root_tokens)

    projected = project(sketch, high, low, activations, depth, rank // rows).reshape(Y, rank // Y, -1)
    projected = jnp.sum(exchange(projected, "row", along_y).astype(jnp.float32), 0)
    projected = projected.astype(jnp.bfloat16).reshape(depth, rank // rows, -1)
    projected = exchange(projected, "row", along_z).astype(jnp.float32)
    projected = jnp.sum(projected, 0) / root_tokens

    width = rank // cols
    first = lax.axis_index("col") * width
    mine = [lax.dynamic_slice_in_dim(part, first, width, 0) for part in (high, low)]
    return (apply_pair(sketch, *mine), projected)


def solution(mesh):
    return jax.shard_map(
        local,
        mesh=mesh,
        in_specs=(P("row", "col"), P("col", None)),
        out_specs=(P("row", "col"), P("row", "col")),
        check_vma=False,
    )
```

```python
import functools
import math

import jax
import jax.numpy as jnp
from jax import lax
from jax.experimental import pallas as pl
from jax.experimental.pallas import tpu as pltpu
from jax.sharding import PartitionSpec as P

Y = 4
PANEL, SUB, LANES = 64, 8, 128
VMEM_BYTES = 58 * 2**20


def groups(rows, cols):
    depth = rows // Y
    plane = [[(z * Y + y) * cols + c for y in range(Y) for c in range(cols)] for z in range(depth)]
    along_z = [[z * Y + y for z in range(depth)] for y in range(Y)]
    along_y = [[z * Y + y for y in range(Y)] for z in range(depth)]
    return plane, along_y, along_z


def exchange(blocks, axis, members=None):
    return lax.all_to_all(blocks, axis, 0, 0, axis_index_groups=members)


def share(block, count, axis, members=None):
    return exchange(jnp.broadcast_to(block[None], (count,) + block.shape), axis, members)


def invert_factor(gram_ref, out_ref, work, scale):
    size = gram_ref.shape[0]
    count, spans = PANEL // SUB, size // LANES
    f32 = jnp.float32
    sub = lax.broadcasted_iota(jnp.int32, (SUB, LANES), 0)
    lanes = lax.broadcasted_iota(jnp.int32, (SUB, LANES), 1)
    work[...] = gram_ref[...]

    def spread(row):
        return jnp.broadcast_to(row, (SUB, LANES))

    def wide(columns):
        return jnp.concatenate([jnp.concatenate([c] * spans, axis=1) for c in columns], axis=0)

    def panel(index, carry):
        start = pl.multiple_of(index * PANEL, PANEL)
        rows = work[pl.ds(start, PANEL), :]
        diagonal = pltpu.roll(rows, (size - start) % size, 1)
        tiles = []
        for g in range(count):
            line = []
            for t in range(spans):
                at = lanes + LANES * t - start
                inside = (at >= 0) & (at < PANEL)
                unit = (at == sub + SUB * g).astype(f32)
                block = rows[SUB * g : SUB * (g + 1), LANES * t : LANES * (t + 1)]
                line.append(jnp.where(inside, unit, block))
            tiles.append(line + [diagonal[SUB * g : SUB * (g + 1), :LANES]])
        inverses, pivots = [], []
        for g in range(count):
            left = range(g, count)
            columns = [
                {h: spread(tiles[h][spans][:, SUB * g + j : SUB * g + j + 1]) for h in left}
                for j in range(SUB)
            ]
            inverse_of, pivot_of = jnp.ones((SUB, LANES), f32), jnp.ones((SUB, LANES), f32)
            for j in range(SUB):
                pivot = spread(columns[j][g][j : j + 1])
                inverse = 1.0 / pivot
                factors = {h: columns[j][h] * inverse for h in left}
                factors[g] = jnp.where(sub > j, factors[g], 0.0)
                for k in range(j + 1, SUB):
                    row = spread(columns[k][g][j : j + 1])
                    for h in left:
                        columns[k][h] = columns[k][h] - factors[h] * row
                for t in range(spans + (g < count - 1)):
                    row = spread(tiles[g][t][j : j + 1])
                    for h in left:
                        tiles[h][t] = tiles[h][t] - factors[h] * row
                inverse_of = jnp.where(sub == j, inverse, inverse_of)
                pivot_of = jnp.where(sub == j, pivot, pivot_of)
            inverses.append(inverse_of)
            pivots.append(pivot_of)
        done = jnp.concatenate([jnp.concatenate(line[:spans], axis=1) for line in tiles], axis=0)
        lane = lax.broadcasted_iota(jnp.int32, (PANEL, size), 1)
        result = done * wide([lax.rsqrt(p) * scale for p in pivots])
        out_ref[pl.ds(start, PANEL), :] = jnp.where(lane < start + PANEL, result, 0.0)
        factors = jnp.where(lane >= start + PANEL, done * wide(inverses), 0.0)
        update = lax.dot_general(
            factors,
            done,
            (((0,), (0,)), ((), ())),
            precision=lax.Precision.HIGHEST,
            preferred_element_type=f32,
        )
        at = lax.broadcasted_iota(jnp.int32, (size, size), 1) - start
        work[...] = jnp.where((at >= 0) & (at < PANEL), 0.0, work[...]) - update
        return carry

    lax.fori_loop(0, size // PANEL, panel, 0)


def split(matrix):
    high = matrix.astype(jnp.bfloat16)
    return high, (matrix - high.astype(jnp.float32)).astype(jnp.bfloat16)


def project_kernel(
    gram_ref, sketch_hbm, activations_hbm, inverse_ref, out_ref,
    work, sketch_ref, activations_ref, done, *, scale, depth, lines,
):
    fetches = [
        pltpu.make_async_copy(sketch_hbm, sketch_ref, done.at[0]),
        pltpu.make_async_copy(activations_hbm, activations_ref, done.at[1]),
    ]
    for fetch in fetches:
        fetch.start()
    invert_factor(gram_ref, inverse_ref, work, scale)
    rank = gram_ref.shape[0]
    f32, bf16 = jnp.float32, jnp.bfloat16
    to = lax.broadcasted_iota(jnp.int32, (rank, rank), 0)
    source = lax.broadcasted_iota(jnp.int32, (rank, rank), 1)
    y, z, line = to // (depth * lines), to // lines % depth, to % lines
    turn = (source == (z * Y + y) * lines + line).astype(bf16)
    by_rows = (((1,), (1,)), ((), ()))
    turned = [
        jnp.dot(turn, part, preferred_element_type=f32).astype(bf16)
        for part in split(inverse_ref[...])
    ]
    fetches[0].wait()
    basis = sum(
        lax.dot_general(part, sketch_ref[...], by_rows, preferred_element_type=f32)
        for part in turned
    ).astype(bf16)
    fetches[1].wait()
    out_ref[...] = jnp.dot(basis, activations_ref[...], preferred_element_type=f32).astype(bf16)


def project(gram, sketch, activations, scale, depth, lines):
    in_vmem, in_hbm = pl.BlockSpec(memory_space=pltpu.VMEM), pl.BlockSpec(memory_space=pltpu.HBM)
    out = jax.ShapeDtypeStruct((gram.shape[0], activations.shape[1]), jnp.bfloat16)
    return pl.pallas_call(
        functools.partial(project_kernel, scale=scale, depth=depth, lines=lines),
        out_shape=[gram, out],
        in_specs=[in_vmem, in_hbm, in_hbm],
        out_specs=[in_vmem, in_vmem],
        scratch_shapes=[
            pltpu.VMEM(gram.shape, jnp.float32),
            pltpu.VMEM(sketch.shape, jnp.bfloat16),
            pltpu.VMEM(activations.shape, jnp.bfloat16),
            pltpu.SemaphoreType.DMA((2,)),
        ],
        compiler_params=pltpu.CompilerParams(vmem_limit_bytes=VMEM_BYTES),
        name="project",
    )(gram, sketch, activations)


def apply_pair(sketch, high, low):
    by_rows = (((1,), (1,)), ((), ()))
    out = lax.dot_general(sketch, high, by_rows, preferred_element_type=jnp.float32)
    out = out + lax.dot_general(sketch, low, by_rows, preferred_element_type=jnp.float32)
    return out.astype(jnp.bfloat16)


def local(activations, start_basis):
    rows, cols = lax.axis_size("row"), lax.axis_size("col")
    rows_dev, rank = activations.shape[0], start_basis.shape[1]
    root_tokens = math.sqrt(rows_dev * rows)
    plane, along_y, along_z = groups(rows, cols)
    plane_size, depth = Y * cols, rows // Y

    partial = jnp.dot(activations, start_basis, preferred_element_type=jnp.float32)
    partial = partial.astype(jnp.bfloat16).reshape(cols, rows_dev // cols, rank)
    parts = exchange(partial, "col")
    own = jnp.sum(parts.astype(jnp.float32), 0).astype(jnp.bfloat16)
    sent = jnp.sum(lax.optimization_barrier(parts).astype(jnp.float32), 0).astype(jnp.bfloat16)
    sketch = lax.all_gather(sent, "col", axis=0, tiled=True)

    gram = lax.dot_general(own, own, (((0,), (0,)), ((), ())), preferred_element_type=jnp.float32)
    gram = gram.reshape(plane_size, rank // plane_size, rank)
    gram = jnp.sum(exchange(gram, ("row", "col"), plane), 0)
    gram = jnp.sum(share(gram, depth, "row", along_z), 0)
    gram = share(gram, plane_size, ("row", "col"), plane).reshape(rank, rank)

    lines = rank // rows
    inverse, projected = project(gram, sketch, activations, root_tokens, depth, lines)
    projected = projected.reshape(Y, rank // Y, -1)
    projected = jnp.sum(exchange(projected, "row", along_y).astype(jnp.float32), 0)
    projected = projected.astype(jnp.bfloat16).reshape(depth, lines, -1)
    projected = exchange(projected, "row", along_z).astype(jnp.float32)
    projected = jnp.sum(projected, 0) / root_tokens

    width = rank // cols
    first = lax.axis_index("col") * width
    mine = split(lax.dynamic_slice_in_dim(inverse, first, width, 0))
    return (apply_pair(sketch, *mine), projected)


def solution(mesh):
    return jax.shard_map(
        local,
        mesh=mesh,
        in_specs=(P("row", "col"), P("col", None)),
        out_specs=(P("row", "col"), P("row", "col")),
        check_vma=False,
    )
```

```python
import functools
import math

import jax
import jax.numpy as jnp
from jax import lax
from jax.experimental import pallas as pl
from jax.experimental.pallas import tpu as pltpu
from jax.sharding import PartitionSpec as P

Y = 4
CORES = 2
PANEL, SUB, LANES = 64, 8, 128
VMEM_BYTES = 58 * 2**20


def groups(rows, cols):
    depth = rows // Y
    plane = [[(z * Y + y) * cols + c for y in range(Y) for c in range(cols)] for z in range(depth)]
    along_z = [[z * Y + y for z in range(depth)] for y in range(Y)]
    along_y = [[z * Y + y for y in range(Y)] for z in range(depth)]
    return plane, along_y, along_z


def exchange(blocks, axis, members=None):
    return lax.all_to_all(blocks, axis, 0, 0, axis_index_groups=members)


def share(block, count, axis, members=None):
    return exchange(jnp.broadcast_to(block[None], (count,) + block.shape), axis, members)


def invert_factor(gram_ref, out_ref, work, scale):
    size = gram_ref.shape[0]
    count, spans = PANEL // SUB, size // LANES
    f32 = jnp.float32
    sub = lax.broadcasted_iota(jnp.int32, (SUB, LANES), 0)
    lanes = lax.broadcasted_iota(jnp.int32, (SUB, LANES), 1)
    work[...] = gram_ref[...]

    def spread(row):
        return jnp.broadcast_to(row, (SUB, LANES))

    def wide(columns):
        return jnp.concatenate([jnp.concatenate([c] * spans, axis=1) for c in columns], axis=0)

    def panel(index, carry):
        start = pl.multiple_of(index * PANEL, PANEL)
        rows = work[pl.ds(start, PANEL), :]
        diagonal = pltpu.roll(rows, (size - start) % size, 1)
        tiles = []
        for g in range(count):
            line = []
            for t in range(spans):
                at = lanes + LANES * t - start
                inside = (at >= 0) & (at < PANEL)
                unit = (at == sub + SUB * g).astype(f32)
                block = rows[SUB * g : SUB * (g + 1), LANES * t : LANES * (t + 1)]
                line.append(jnp.where(inside, unit, block))
            tiles.append(line + [diagonal[SUB * g : SUB * (g + 1), :LANES]])
        inverses, pivots = [], []
        for g in range(count):
            left = range(g, count)
            columns = [
                {h: spread(tiles[h][spans][:, SUB * g + j : SUB * g + j + 1]) for h in left}
                for j in range(SUB)
            ]
            inverse_of, pivot_of = jnp.ones((SUB, LANES), f32), jnp.ones((SUB, LANES), f32)
            for j in range(SUB):
                pivot = spread(columns[j][g][j : j + 1])
                inverse = 1.0 / pivot
                factors = {h: columns[j][h] * inverse for h in left}
                factors[g] = jnp.where(sub > j, factors[g], 0.0)
                for k in range(j + 1, SUB):
                    row = spread(columns[k][g][j : j + 1])
                    for h in left:
                        columns[k][h] = columns[k][h] - factors[h] * row
                for t in range(spans + (g < count - 1)):
                    row = spread(tiles[g][t][j : j + 1])
                    for h in left:
                        tiles[h][t] = tiles[h][t] - factors[h] * row
                inverse_of = jnp.where(sub == j, inverse, inverse_of)
                pivot_of = jnp.where(sub == j, pivot, pivot_of)
            inverses.append(inverse_of)
            pivots.append(pivot_of)
        done = jnp.concatenate([jnp.concatenate(line[:spans], axis=1) for line in tiles], axis=0)
        lane = lax.broadcasted_iota(jnp.int32, (PANEL, size), 1)
        result = done * wide([lax.rsqrt(p) * scale for p in pivots])
        out_ref[pl.ds(start, PANEL), :] = jnp.where(lane < start + PANEL, result, 0.0)
        factors = jnp.where(lane >= start + PANEL, done * wide(inverses), 0.0)
        update = lax.dot_general(
            factors,
            done,
            (((0,), (0,)), ((), ())),
            precision=lax.Precision.HIGHEST,
            preferred_element_type=f32,
        )
        at = lax.broadcasted_iota(jnp.int32, (size, size), 1) - start
        work[...] = jnp.where((at >= 0) & (at < PANEL), 0.0, work[...]) - update
        return carry

    lax.fori_loop(0, size // PANEL, panel, 0)


def split(matrix):
    high = matrix.astype(jnp.bfloat16)
    return high, (matrix - high.astype(jnp.float32)).astype(jnp.bfloat16)


def project_kernel(
    gram_ref, near_hbm, far_hbm, activations_hbm, basis_ref, out_ref,
    work, inverse_ref, sketch_ref, activations_ref, done, *, scale, depth, lines,
):
    col = lax.axis_index("col")
    chips, tokens = near_hbm.shape[:2]
    chip, core = col // CORES, col % CORES
    fetches = []
    for step in range(chips):
        for other, slices in enumerate((near_hbm, far_hbm)):
            place = (chip + step) % chips * CORES + (core + other) % CORES
            rows = pl.ds(pl.multiple_of(place * tokens, tokens), tokens)
            at = done.at[CORES * step + other]
            fetches.append(pltpu.make_async_copy(slices.at[step], sketch_ref.at[rows], at))
    last = pltpu.make_async_copy(activations_hbm, activations_ref, done.at[CORES * chips])
    for fetch in fetches:
        fetch.start()
    last.start()
    invert_factor(gram_ref, inverse_ref, work, scale)
    rank = gram_ref.shape[0]
    f32, bf16 = jnp.float32, jnp.bfloat16
    to = lax.broadcasted_iota(jnp.int32, (rank, rank), 0)
    source = lax.broadcasted_iota(jnp.int32, (rank, rank), 1)
    y, z, line = to // (depth * lines), to // lines % depth, to % lines
    turn = (source == (z * Y + y) * lines + line).astype(bf16)
    turned = [
        jnp.dot(turn, part, preferred_element_type=f32).astype(bf16)
        for part in split(inverse_ref[...])
    ]
    for fetch in fetches:
        fetch.wait()

    def basis_of(parts):
        by_rows = (((1,), (1,)), ((), ()))
        terms = [
            lax.dot_general(part, sketch_ref[...], by_rows, preferred_element_type=f32)
            for part in parts
        ]
        return (terms[0] + terms[1]).astype(bf16)

    width = basis_ref.shape[0]
    mine = inverse_ref[pl.ds(pl.multiple_of(col * width, width), width), :]
    basis_ref[...] = basis_of(split(mine))
    basis = basis_of(turned)
    last.wait()
    out_ref[...] = jnp.dot(basis, activations_ref[...], preferred_element_type=f32).astype(bf16)


def project(gram, near, far, activations, scale, depth, lines):
    in_vmem, in_hbm = pl.BlockSpec(memory_space=pltpu.VMEM), pl.BlockSpec(memory_space=pltpu.HBM)
    rank, cols = gram.shape[0], lax.axis_size("col")
    tokens, features = activations.shape
    return pl.pallas_call(
        functools.partial(project_kernel, scale=scale, depth=depth, lines=lines),
        out_shape=[
            jax.ShapeDtypeStruct((rank // cols, tokens), jnp.bfloat16),
            jax.ShapeDtypeStruct((rank, features), jnp.bfloat16),
        ],
        in_specs=[in_vmem, in_hbm, in_hbm, in_hbm],
        out_specs=[in_vmem, in_vmem],
        scratch_shapes=[
            pltpu.VMEM(gram.shape, jnp.float32),
            pltpu.VMEM(gram.shape, jnp.float32),
            pltpu.VMEM((tokens, rank), jnp.bfloat16),
            pltpu.VMEM(activations.shape, jnp.bfloat16),
            pltpu.SemaphoreType.DMA((cols + 1,)),
        ],
        compiler_params=pltpu.CompilerParams(vmem_limit_bytes=VMEM_BYTES),
        name="project",
    )(gram, near, far, activations)


def gather_sketch(own):
    cols = lax.axis_size("col")
    chips = cols // CORES
    near = [own]
    for step in range(1, chips):
        pairs = [(c, (c - CORES * step) % cols) for c in range(cols)]
        near.append(lax.ppermute(own, "col", pairs))
    near = jnp.stack(near)
    far = lax.ppermute(near, "col", [(c, c ^ 1) for c in range(cols)])
    return near, far


def local(activations, start_basis):
    rows, cols = lax.axis_size("row"), lax.axis_size("col")
    rows_dev, rank = activations.shape[0], start_basis.shape[1]
    root_tokens = math.sqrt(rows_dev * rows)
    plane, along_y, along_z = groups(rows, cols)
    plane_size, depth = Y * cols, rows // Y

    partial = jnp.dot(activations, start_basis, preferred_element_type=jnp.float32)
    partial = partial.astype(jnp.bfloat16).reshape(cols, rows_dev // cols, rank)
    parts = exchange(partial, "col")
    own = jnp.sum(parts.astype(jnp.float32), 0).astype(jnp.bfloat16)
    near, far = gather_sketch(own)

    gram = lax.dot_general(own, own, (((0,), (0,)), ((), ())), preferred_element_type=jnp.float32)
    gram = gram.reshape(plane_size, rank // plane_size, rank)
    gram = jnp.sum(exchange(gram, ("row", "col"), plane), 0)
    gram = jnp.sum(share(gram, depth, "row", along_z), 0)
    gram = share(gram, plane_size, ("row", "col"), plane).reshape(rank, rank)

    lines = rank // rows
    basis, projected = project(gram, near, far, activations, root_tokens, depth, lines)
    projected = projected.reshape(Y, rank // Y, -1)
    projected = jnp.sum(exchange(projected, "row", along_y).astype(jnp.float32), 0)
    projected = projected.astype(jnp.bfloat16).reshape(depth, lines, -1)
    projected = exchange(projected, "row", along_z).astype(jnp.float32)
    projected = jnp.sum(projected, 0) / root_tokens

    return (basis.T, projected)


def solution(mesh):
    return jax.shard_map(
        local,
        mesh=mesh,
        in_specs=(P("row", "col"), P("col", None)),
        out_specs=(P("row", "col"), P("row", "col")),
        check_vma=False,
    )
```

```python
import functools
import math

import jax
import jax.numpy as jnp
from jax import lax
from jax.experimental import pallas as pl
from jax.experimental.pallas import tpu as pltpu
from jax.sharding import PartitionSpec as P

Y = 4
CORES = 2
PANEL, SUB, LANES = 64, 8, 128
VMEM_BYTES = 58 * 2**20


def groups(rows, cols):
    depth = rows // Y
    plane = [[(z * Y + y) * cols + c for y in range(Y) for c in range(cols)] for z in range(depth)]
    along_z = [[z * Y + y for z in range(depth)] for y in range(Y)]
    along_y = [[z * Y + y for y in range(Y)] for z in range(depth)]
    along_x = [list(range(core, cols, CORES)) for core in range(CORES)]
    return plane, along_x, along_y, along_z


def exchange(blocks, axis, members=None):
    return lax.all_to_all(blocks, axis, 0, 0, axis_index_groups=members)


def share(block, count, axis, members=None):
    return exchange(jnp.broadcast_to(block[None], (count,) + block.shape), axis, members)


def invert_factor(gram_ref, out_ref, work, scale):
    size = gram_ref.shape[0]
    count, spans = PANEL // SUB, size // LANES
    f32 = jnp.float32
    sub = lax.broadcasted_iota(jnp.int32, (SUB, LANES), 0)
    lanes = lax.broadcasted_iota(jnp.int32, (SUB, LANES), 1)
    work[...] = gram_ref[...]

    def spread(row):
        return jnp.broadcast_to(row, (SUB, LANES))

    def wide(columns):
        return jnp.concatenate([jnp.concatenate([c] * spans, axis=1) for c in columns], axis=0)

    def panel(index, carry):
        start = pl.multiple_of(index * PANEL, PANEL)
        rows = work[pl.ds(start, PANEL), :]
        diagonal = pltpu.roll(rows, (size - start) % size, 1)
        tiles = []
        for g in range(count):
            line = []
            for t in range(spans):
                at = lanes + LANES * t - start
                inside = (at >= 0) & (at < PANEL)
                unit = (at == sub + SUB * g).astype(f32)
                block = rows[SUB * g : SUB * (g + 1), LANES * t : LANES * (t + 1)]
                line.append(jnp.where(inside, unit, block))
            tiles.append(line + [diagonal[SUB * g : SUB * (g + 1), :LANES]])
        inverses, pivots = [], []
        for g in range(count):
            left = range(g, count)
            columns = [
                {h: spread(tiles[h][spans][:, SUB * g + j : SUB * g + j + 1]) for h in left}
                for j in range(SUB)
            ]
            inverse_of, pivot_of = jnp.ones((SUB, LANES), f32), jnp.ones((SUB, LANES), f32)
            for j in range(SUB):
                pivot = spread(columns[j][g][j : j + 1])
                inverse = 1.0 / pivot
                factors = {h: columns[j][h] * inverse for h in left}
                factors[g] = jnp.where(sub > j, factors[g], 0.0)
                for k in range(j + 1, SUB):
                    row = spread(columns[k][g][j : j + 1])
                    for h in left:
                        columns[k][h] = columns[k][h] - factors[h] * row
                for t in range(spans + (g < count - 1)):
                    row = spread(tiles[g][t][j : j + 1])
                    for h in left:
                        tiles[h][t] = tiles[h][t] - factors[h] * row
                inverse_of = jnp.where(sub == j, inverse, inverse_of)
                pivot_of = jnp.where(sub == j, pivot, pivot_of)
            inverses.append(inverse_of)
            pivots.append(pivot_of)
        done = jnp.concatenate([jnp.concatenate(line[:spans], axis=1) for line in tiles], axis=0)
        lane = lax.broadcasted_iota(jnp.int32, (PANEL, size), 1)
        result = done * wide([lax.rsqrt(p) * scale for p in pivots])
        out_ref[pl.ds(start, PANEL), :] = jnp.where(lane < start + PANEL, result, 0.0)
        factors = jnp.where(lane >= start + PANEL, done * wide(inverses), 0.0)
        update = lax.dot_general(
            factors,
            done,
            (((0,), (0,)), ((), ())),
            precision=lax.Precision.HIGHEST,
            preferred_element_type=f32,
        )
        at = lax.broadcasted_iota(jnp.int32, (size, size), 1) - start
        work[...] = jnp.where((at >= 0) & (at < PANEL), 0.0, work[...]) - update
        return carry

    lax.fori_loop(0, size // PANEL, panel, 0)


def split(matrix):
    high = matrix.astype(jnp.bfloat16)
    return high, (matrix - high.astype(jnp.float32)).astype(jnp.bfloat16)


def project_kernel(
    gram_ref, near_hbm, far_hbm, activations_hbm, basis_ref, out_ref,
    work, inverse_ref, sketch_ref, activations_ref, done, *, scale, depth, lines,
):
    col = lax.axis_index("col")
    chips, tokens = near_hbm.shape[:2]
    chip, core = col // CORES, col % CORES
    fetches = []
    for step in range(chips):
        for other, slices in enumerate((near_hbm, far_hbm)):
            place = (core + other) % CORES * chips + (chip + step) % chips
            rows = pl.ds(pl.multiple_of(place * tokens, tokens), tokens)
            at = done.at[CORES * step + other]
            fetches.append(pltpu.make_async_copy(slices.at[step], sketch_ref.at[rows], at))
    last = pltpu.make_async_copy(activations_hbm, activations_ref, done.at[CORES * chips])
    for fetch in fetches:
        fetch.start()
    last.start()
    invert_factor(gram_ref, inverse_ref, work, scale)
    rank = gram_ref.shape[0]
    f32, bf16 = jnp.float32, jnp.bfloat16
    to = lax.broadcasted_iota(jnp.int32, (rank, rank), 0)
    source = lax.broadcasted_iota(jnp.int32, (rank, rank), 1)
    y, z, line = to // (depth * lines), to // lines % depth, to % lines
    turn = (source == (z * Y + y) * lines + line).astype(bf16)
    turned = [
        jnp.dot(turn, part, preferred_element_type=f32).astype(bf16)
        for part in split(inverse_ref[...])
    ]
    for fetch in fetches:
        fetch.wait()

    def basis_of(parts):
        by_rows = (((1,), (1,)), ((), ()))
        terms = [
            lax.dot_general(part, sketch_ref[...], by_rows, preferred_element_type=f32)
            for part in parts
        ]
        return (terms[0] + terms[1]).astype(bf16)

    width = basis_ref.shape[0]
    mine = inverse_ref[pl.ds(pl.multiple_of(col * width, width), width), :]
    basis_ref[...] = basis_of(split(mine))
    basis = basis_of(turned)
    last.wait()
    out_ref[...] = jnp.dot(basis, activations_ref[...], preferred_element_type=f32).astype(bf16)


def project(gram, near, far, activations, scale, depth, lines):
    in_vmem, in_hbm = pl.BlockSpec(memory_space=pltpu.VMEM), pl.BlockSpec(memory_space=pltpu.HBM)
    rank, cols = gram.shape[0], lax.axis_size("col")
    tokens, features = activations.shape
    return pl.pallas_call(
        functools.partial(project_kernel, scale=scale, depth=depth, lines=lines),
        out_shape=[
            jax.ShapeDtypeStruct((rank // cols, tokens), jnp.bfloat16),
            jax.ShapeDtypeStruct((rank, features), jnp.bfloat16),
        ],
        in_specs=[in_vmem, in_hbm, in_hbm, in_hbm],
        out_specs=[in_vmem, in_vmem],
        scratch_shapes=[
            pltpu.VMEM(gram.shape, jnp.float32),
            pltpu.VMEM(gram.shape, jnp.float32),
            pltpu.VMEM((tokens, rank), jnp.bfloat16),
            pltpu.VMEM(activations.shape, jnp.bfloat16),
            pltpu.SemaphoreType.DMA((cols + 1,)),
        ],
        compiler_params=pltpu.CompilerParams(vmem_limit_bytes=VMEM_BYTES),
        name="project",
    )(gram, near, far, activations)


def from_chip(own, step):
    cols = lax.axis_size("col")
    return lax.ppermute(own, "col", [(c, (c - CORES * step) % cols) for c in range(cols)])


def local(activations, start_basis):
    rows, cols = lax.axis_size("row"), lax.axis_size("col")
    rows_dev, rank = activations.shape[0], start_basis.shape[1]
    root_tokens = math.sqrt(rows_dev * rows)
    plane, along_x, along_y, along_z = groups(rows, cols)
    plane_size, depth = Y * cols, rows // Y

    half, core = rows_dev // CORES, lax.axis_index("col") % CORES

    def half_sketch(index):
        block = lax.dynamic_slice_in_dim(activations, index * half, half, 0)
        return jnp.dot(block, start_basis, preferred_element_type=jnp.float32)

    other = half_sketch(1 - core).astype(jnp.bfloat16)
    other = lax.ppermute(other, "col", [(c, c ^ 1) for c in range(cols)])
    mine = lax.optimization_barrier(half_sketch(core))
    partial = (mine + other.astype(jnp.float32)).astype(jnp.bfloat16)
    partial = partial.reshape(cols // CORES, -1, rank)
    parts = exchange(partial, "col", along_x)
    own = jnp.sum(parts.astype(jnp.float32), 0).astype(jnp.bfloat16)
    first_near = [own] + [from_chip(own, step) for step in range(1, cols // CORES - 1)]

    gram = lax.dot_general(own, own, (((0,), (0,)), ((), ())), preferred_element_type=jnp.float32)
    gram = gram.reshape(plane_size, rank // plane_size, rank)
    gram = jnp.sum(exchange(gram, ("row", "col"), plane), 0)
    late, _ = lax.optimization_barrier((own, gram))
    near = jnp.stack(first_near + [from_chip(late, cols // CORES - 1)])
    far = lax.ppermute(near, "col", [(c, c ^ 1) for c in range(cols)])
    gram = jnp.sum(share(gram, depth, "row", along_z), 0)
    gram = share(gram, plane_size, ("row", "col"), plane).reshape(rank, rank)

    lines = rank // rows
    basis, projected = project(gram, near, far, activations, root_tokens, depth, lines)
    projected = projected.reshape(Y, rank // Y, -1)
    projected = jnp.sum(exchange(projected, "row", along_y).astype(jnp.float32), 0)
    projected = projected.astype(jnp.bfloat16).reshape(depth, lines, -1)
    projected = exchange(projected, "row", along_z).astype(jnp.float32)
    projected = jnp.sum(projected, 0) / root_tokens

    return (basis.T, projected)


def solution(mesh):
    return jax.shard_map(
        local,
        mesh=mesh,
        in_specs=(P("row", "col"), P("col", None)),
        out_specs=(P("row", "col"), P("row", "col")),
        check_vma=False,
    )
```

```python
import functools
import math

import jax
import jax.numpy as jnp
from jax import lax
from jax.experimental import pallas as pl
from jax.experimental.pallas import tpu as pltpu
from jax.sharding import PartitionSpec as P

Y = 4
CORES = 2
PANEL, SUB, LANES = 64, 8, 128
VMEM_BYTES = 52 * 2**20


def groups(rows, cols):
    depth = rows // Y
    plane = [[(z * Y + y) * cols + c for y in range(Y) for c in range(cols)] for z in range(depth)]
    along_z = [[z * Y + y for z in range(depth)] for y in range(Y)]
    along_y = [[z * Y + y for y in range(Y)] for z in range(depth)]
    along_x = [list(range(core, cols, CORES)) for core in range(CORES)]
    return plane, along_x, along_y, along_z


def exchange(blocks, axis, members=None):
    return lax.all_to_all(blocks, axis, 0, 0, axis_index_groups=members)


def share(block, count, axis, members=None):
    return exchange(jnp.broadcast_to(block[None], (count,) + block.shape), axis, members)


def invert_factor(gram_ref, out_ref, work, scale):
    size = gram_ref.shape[0]
    count, spans = PANEL // SUB, size // LANES
    f32 = jnp.float32
    sub = lax.broadcasted_iota(jnp.int32, (SUB, LANES), 0)
    lanes = lax.broadcasted_iota(jnp.int32, (SUB, LANES), 1)
    work[...] = gram_ref[...]

    def spread(row):
        return jnp.broadcast_to(row, (SUB, LANES))

    def wide(columns):
        return jnp.concatenate([jnp.concatenate([c] * spans, axis=1) for c in columns], axis=0)

    def panel(index, carry):
        start = pl.multiple_of(index * PANEL, PANEL)
        rows = work[pl.ds(start, PANEL), :]
        diagonal = pltpu.roll(rows, (size - start) % size, 1)
        tiles = []
        for g in range(count):
            line = []
            for t in range(spans):
                at = lanes + LANES * t - start
                inside = (at >= 0) & (at < PANEL)
                unit = (at == sub + SUB * g).astype(f32)
                block = rows[SUB * g : SUB * (g + 1), LANES * t : LANES * (t + 1)]
                line.append(jnp.where(inside, unit, block))
            tiles.append(line + [diagonal[SUB * g : SUB * (g + 1), :LANES]])
        inverses, pivots = [], []
        for g in range(count):
            left = range(g, count)
            columns = [
                {h: spread(tiles[h][spans][:, SUB * g + j : SUB * g + j + 1]) for h in left}
                for j in range(SUB)
            ]
            inverse_of, pivot_of = jnp.ones((SUB, LANES), f32), jnp.ones((SUB, LANES), f32)
            for j in range(SUB):
                pivot = spread(columns[j][g][j : j + 1])
                inverse = 1.0 / pivot
                factors = {h: columns[j][h] * inverse for h in left}
                factors[g] = jnp.where(sub > j, factors[g], 0.0)
                for k in range(j + 1, SUB):
                    row = spread(columns[k][g][j : j + 1])
                    for h in left:
                        columns[k][h] = columns[k][h] - factors[h] * row
                for t in range(spans + (g < count - 1)):
                    row = spread(tiles[g][t][j : j + 1])
                    for h in left:
                        tiles[h][t] = tiles[h][t] - factors[h] * row
                inverse_of = jnp.where(sub == j, inverse, inverse_of)
                pivot_of = jnp.where(sub == j, pivot, pivot_of)
            inverses.append(inverse_of)
            pivots.append(pivot_of)
        done = jnp.concatenate([jnp.concatenate(line[:spans], axis=1) for line in tiles], axis=0)
        lane = lax.broadcasted_iota(jnp.int32, (PANEL, size), 1)
        result = done * wide([lax.rsqrt(p) * scale for p in pivots])
        out_ref[pl.ds(start, PANEL), :] = jnp.where(lane < start + PANEL, result, 0.0)
        factors = jnp.where(lane >= start + PANEL, done * wide(inverses), 0.0)
        update = lax.dot_general(
            factors,
            done,
            (((0,), (0,)), ((), ())),
            precision=lax.Precision.HIGHEST,
            preferred_element_type=f32,
        )
        at = lax.broadcasted_iota(jnp.int32, (size, size), 1) - start
        work[...] = jnp.where((at >= 0) & (at < PANEL), 0.0, work[...]) - update
        return carry

    lax.fori_loop(0, size // PANEL, panel, 0)


def split(matrix):
    high = matrix.astype(jnp.bfloat16)
    return high, (matrix - high.astype(jnp.float32)).astype(jnp.bfloat16)


def project_kernel(
    gram_ref, near_hbm, far_hbm, activations_hbm, basis_ref, out_ref,
    work, inverse_ref, sketch_ref, activations_ref, done, *, scale, depth, lines,
):
    col = lax.axis_index("col")
    chips, tokens = near_hbm.shape[:2]
    chip, core = col // CORES, col % CORES
    fetches = []
    for step in range(chips):
        for other, slices in enumerate((near_hbm, far_hbm)):
            place = (core + other) % CORES * chips + (chip + step) % chips
            rows = pl.ds(pl.multiple_of(place * tokens, tokens), tokens)
            at = done.at[CORES * step + other]
            fetches.append(pltpu.make_async_copy(slices.at[step], sketch_ref.at[rows], at))
    last = pltpu.make_async_copy(activations_hbm, activations_ref, done.at[CORES * chips])
    for fetch in fetches:
        fetch.start()
    last.start()
    invert_factor(gram_ref, inverse_ref, work, scale)
    rank = gram_ref.shape[0]
    f32, bf16 = jnp.float32, jnp.bfloat16
    to = lax.broadcasted_iota(jnp.int32, (rank, rank), 0)
    source = lax.broadcasted_iota(jnp.int32, (rank, rank), 1)
    y, z, line = to // (depth * lines), to // lines % depth, to % lines
    turn = (source == (z * Y + y) * lines + line).astype(bf16)
    turned = [
        jnp.dot(turn, part, preferred_element_type=f32).astype(bf16)
        for part in split(inverse_ref[...])
    ]
    for fetch in fetches:
        fetch.wait()

    def basis_of(parts):
        by_rows = (((1,), (1,)), ((), ()))
        terms = [
            lax.dot_general(part, sketch_ref[...], by_rows, preferred_element_type=f32)
            for part in parts
        ]
        return (terms[0] + terms[1]).astype(bf16)

    width = basis_ref.shape[0]
    mine = inverse_ref[pl.ds(pl.multiple_of(col * width, width), width), :]
    basis_ref[...] = basis_of(split(mine))
    basis = basis_of(turned)
    last.wait()
    projected = jnp.dot(basis, activations_ref[...], preferred_element_type=f32)
    out_ref[...] = (projected * (1.0 / scale)).astype(bf16)


def project(gram, near, far, activations, scale, depth, lines):
    in_vmem, in_hbm = pl.BlockSpec(memory_space=pltpu.VMEM), pl.BlockSpec(memory_space=pltpu.HBM)
    rank, cols = gram.shape[0], lax.axis_size("col")
    tokens, features = activations.shape
    return pl.pallas_call(
        functools.partial(project_kernel, scale=scale, depth=depth, lines=lines),
        out_shape=[
            jax.ShapeDtypeStruct((rank // cols, tokens), jnp.bfloat16),
            jax.ShapeDtypeStruct((rank, features), jnp.bfloat16),
        ],
        in_specs=[in_vmem, in_hbm, in_hbm, in_hbm],
        out_specs=[in_vmem, in_vmem],
        scratch_shapes=[
            pltpu.VMEM(gram.shape, jnp.float32),
            pltpu.VMEM(gram.shape, jnp.float32),
            pltpu.VMEM((tokens, rank), jnp.bfloat16),
            pltpu.VMEM(activations.shape, jnp.bfloat16),
            pltpu.SemaphoreType.DMA((cols + 1,)),
        ],
        compiler_params=pltpu.CompilerParams(vmem_limit_bytes=VMEM_BYTES),
        name="project",
    )(gram, near, far, activations)


def from_chip(own, step):
    cols = lax.axis_size("col")
    return lax.ppermute(own, "col", [(c, (c - CORES * step) % cols) for c in range(cols)])


def local(activations, start_basis):
    rows, cols = lax.axis_size("row"), lax.axis_size("col")
    rows_dev, rank = activations.shape[0], start_basis.shape[1]
    root_tokens = math.sqrt(rows_dev * rows)
    plane, along_x, along_y, along_z = groups(rows, cols)
    plane_size, depth = Y * cols, rows // Y

    half, core = rows_dev // CORES, lax.axis_index("col") % CORES

    def half_sketch(index):
        block = lax.dynamic_slice_in_dim(activations, index * half, half, 0)
        return jnp.dot(block, start_basis, preferred_element_type=jnp.float32)

    other = half_sketch(1 - core).astype(jnp.bfloat16)
    other = lax.ppermute(other, "col", [(c, c ^ 1) for c in range(cols)])
    mine = lax.optimization_barrier(half_sketch(core))
    partial = (mine + other.astype(jnp.float32)).astype(jnp.bfloat16)
    partial = partial.reshape(cols // CORES, -1, rank)
    parts = exchange(partial, "col", along_x)
    own = jnp.sum(parts.astype(jnp.float32), 0).astype(jnp.bfloat16)
    first_near = [own] + [from_chip(own, step) for step in range(1, cols // CORES - 1)]

    gram = lax.dot_general(own, own, (((0,), (0,)), ((), ())), preferred_element_type=jnp.float32)
    gram = gram.reshape(plane_size, rank // plane_size, rank)
    gram = jnp.sum(exchange(gram, ("row", "col"), plane), 0)
    late, _ = lax.optimization_barrier((own, gram))
    near = jnp.stack(first_near + [from_chip(late, cols // CORES - 1)])
    far = lax.ppermute(near, "col", [(c, c ^ 1) for c in range(cols)])
    gram = jnp.sum(share(gram, depth, "row", along_z), 0)
    gram = share(gram, plane_size, ("row", "col"), plane).reshape(rank, rank)

    lines = rank // rows
    basis, projected = project(gram, near, far, activations, root_tokens, depth, lines)
    projected = projected.reshape(Y, rank // Y, -1)
    projected = jnp.sum(exchange(projected, "row", along_y).astype(jnp.float32), 0)
    projected = projected.astype(jnp.bfloat16).reshape(depth, lines, -1)
    projected = exchange(projected, "row", along_z).astype(jnp.float32)
    projected = jnp.sum(projected, 0)

    return (basis.T, projected)


def solution(mesh):
    return jax.shard_map(
        local,
        mesh=mesh,
        in_specs=(P("row", "col"), P("col", None)),
        out_specs=(P("row", "col"), P("row", "col")),
        check_vma=False,
    )
```

```python
import functools
import math

import jax
import jax.numpy as jnp
from jax import lax
from jax.experimental import pallas as pl
from jax.experimental.pallas import tpu as pltpu
from jax.sharding import PartitionSpec as P

Y = 4
CORES = 2
PANEL, SUB, LANES = 64, 8, 128
VMEM_BYTES = 52 * 2**20


def groups(rows, cols):
    depth = rows // Y
    plane = [[(z * Y + y) * cols + c for y in range(Y) for c in range(cols)] for z in range(depth)]
    along_z = [[z * Y + y for z in range(depth)] for y in range(Y)]
    along_y = [[z * Y + y for y in range(Y)] for z in range(depth)]
    along_x = [list(range(core, cols, CORES)) for core in range(CORES)]
    return plane, along_x, along_y, along_z


def exchange(blocks, axis, members=None):
    return lax.all_to_all(blocks, axis, 0, 0, axis_index_groups=members)


def share(block, count, axis, members=None):
    return exchange(jnp.broadcast_to(block[None], (count,) + block.shape), axis, members)


def invert_factor(gram_ref, out_ref, work, scale):
    size = gram_ref.shape[0]
    count, spans = PANEL // SUB, size // LANES
    f32 = jnp.float32
    sub = lax.broadcasted_iota(jnp.int32, (SUB, LANES), 0)
    lanes = lax.broadcasted_iota(jnp.int32, (SUB, LANES), 1)
    work[...] = gram_ref[...]

    def spread(row):
        return jnp.broadcast_to(row, (SUB, LANES))

    def wide(columns):
        return jnp.concatenate([jnp.concatenate([c] * spans, axis=1) for c in columns], axis=0)

    def panel(index, carry):
        start = pl.multiple_of(index * PANEL, PANEL)
        rows = work[pl.ds(start, PANEL), :]
        diagonal = pltpu.roll(rows, (size - start) % size, 1)
        tiles = []
        for g in range(count):
            line = []
            for t in range(spans):
                at = lanes + LANES * t - start
                inside = (at >= 0) & (at < PANEL)
                unit = (at == sub + SUB * g).astype(f32)
                block = rows[SUB * g : SUB * (g + 1), LANES * t : LANES * (t + 1)]
                line.append(jnp.where(inside, unit, block))
            tiles.append(line + [diagonal[SUB * g : SUB * (g + 1), :LANES]])
        inverses, pivots = [], []
        for g in range(count):
            left = range(g, count)
            columns = [
                {h: spread(tiles[h][spans][:, SUB * g + j : SUB * g + j + 1]) for h in left}
                for j in range(SUB)
            ]
            inverse_of, pivot_of = jnp.ones((SUB, LANES), f32), jnp.ones((SUB, LANES), f32)
            for j in range(SUB):
                pivot = spread(columns[j][g][j : j + 1])
                inverse = 1.0 / pivot
                factors = {h: columns[j][h] * inverse for h in left}
                factors[g] = jnp.where(sub > j, factors[g], 0.0)
                for k in range(j + 1, SUB):
                    row = spread(columns[k][g][j : j + 1])
                    for h in left:
                        columns[k][h] = columns[k][h] - factors[h] * row
                for t in range(spans + (g < count - 1)):
                    row = spread(tiles[g][t][j : j + 1])
                    for h in left:
                        tiles[h][t] = tiles[h][t] - factors[h] * row
                inverse_of = jnp.where(sub == j, inverse, inverse_of)
                pivot_of = jnp.where(sub == j, pivot, pivot_of)
            inverses.append(inverse_of)
            pivots.append(pivot_of)
        done = jnp.concatenate([jnp.concatenate(line[:spans], axis=1) for line in tiles], axis=0)
        lane = lax.broadcasted_iota(jnp.int32, (PANEL, size), 1)
        result = done * wide([lax.rsqrt(p) * scale for p in pivots])
        out_ref[pl.ds(start, PANEL), :] = jnp.where(lane < start + PANEL, result, 0.0)
        factors = jnp.where(lane >= start + PANEL, done * wide(inverses), 0.0)
        update = lax.dot_general(
            factors,
            done,
            (((0,), (0,)), ((), ())),
            precision=lax.Precision.HIGHEST,
            preferred_element_type=f32,
        )
        at = lax.broadcasted_iota(jnp.int32, (size, size), 1) - start
        work[...] = jnp.where((at >= 0) & (at < PANEL), 0.0, work[...]) - update
        return carry

    lax.fori_loop(0, size // PANEL, panel, 0)


def split(matrix):
    high = matrix.astype(jnp.bfloat16)
    return high, (matrix - high.astype(jnp.float32)).astype(jnp.bfloat16)


def project_kernel(
    gram_ref, near_hbm, far_hbm, activations_hbm, basis_ref, out_ref,
    work, inverse_ref, sketch_ref, activations_ref, done, *, scale, depth, lines,
):
    col = lax.axis_index("col")
    chips, tokens = near_hbm.shape[:2]
    chip, core = col // CORES, col % CORES
    fetches = []
    for step in range(chips):
        for other, slices in enumerate((near_hbm, far_hbm)):
            place = (core + other) % CORES * chips + (chip ^ step)
            rows = pl.ds(pl.multiple_of(place * tokens, tokens), tokens)
            at = done.at[CORES * step + other]
            fetches.append(pltpu.make_async_copy(slices.at[step], sketch_ref.at[rows], at))
    last = pltpu.make_async_copy(activations_hbm, activations_ref, done.at[CORES * chips])
    for fetch in fetches:
        fetch.start()
    last.start()
    invert_factor(gram_ref, inverse_ref, work, scale)
    rank = gram_ref.shape[0]
    f32, bf16 = jnp.float32, jnp.bfloat16
    to = lax.broadcasted_iota(jnp.int32, (rank, rank), 0)
    source = lax.broadcasted_iota(jnp.int32, (rank, rank), 1)
    y, z, line = to // (depth * lines), to // lines % depth, to % lines
    turn = (source == (z * Y + y) * lines + line).astype(bf16)
    turned = [
        jnp.dot(turn, part, preferred_element_type=f32).astype(bf16)
        for part in split(inverse_ref[...])
    ]
    for fetch in fetches:
        fetch.wait()

    def basis_of(parts):
        by_rows = (((1,), (1,)), ((), ()))
        terms = [
            lax.dot_general(part, sketch_ref[...], by_rows, preferred_element_type=f32)
            for part in parts
        ]
        return (terms[0] + terms[1]).astype(bf16)

    width = basis_ref.shape[0]
    mine = inverse_ref[pl.ds(pl.multiple_of(col * width, width), width), :]
    basis_ref[...] = basis_of(split(mine))
    basis = basis_of(turned)
    last.wait()
    projected = jnp.dot(basis, activations_ref[...], preferred_element_type=f32)
    out_ref[...] = (projected * (1.0 / scale)).astype(bf16)


def project(gram, near, far, activations, scale, depth, lines):
    in_vmem, in_hbm = pl.BlockSpec(memory_space=pltpu.VMEM), pl.BlockSpec(memory_space=pltpu.HBM)
    rank, cols = gram.shape[0], lax.axis_size("col")
    tokens, features = activations.shape
    return pl.pallas_call(
        functools.partial(project_kernel, scale=scale, depth=depth, lines=lines),
        out_shape=[
            jax.ShapeDtypeStruct((rank // cols, tokens), jnp.bfloat16),
            jax.ShapeDtypeStruct((rank, features), jnp.bfloat16),
        ],
        in_specs=[in_vmem, in_hbm, in_hbm, in_hbm],
        out_specs=[in_vmem, in_vmem],
        scratch_shapes=[
            pltpu.VMEM(gram.shape, jnp.float32),
            pltpu.VMEM(gram.shape, jnp.float32),
            pltpu.VMEM((tokens, rank), jnp.bfloat16),
            pltpu.VMEM(activations.shape, jnp.bfloat16),
            pltpu.SemaphoreType.DMA((cols + 1,)),
        ],
        compiler_params=pltpu.CompilerParams(vmem_limit_bytes=VMEM_BYTES),
        name="project",
    )(gram, near, far, activations)


def swap(slices, distance):
    return lax.ppermute(slices, "col", [(c, c ^ distance) for c in range(lax.axis_size("col"))])


def local(activations, start_basis):
    rows, cols = lax.axis_size("row"), lax.axis_size("col")
    rows_dev, rank = activations.shape[0], start_basis.shape[1]
    root_tokens = math.sqrt(rows_dev * rows)
    plane, along_x, along_y, along_z = groups(rows, cols)
    plane_size, depth = Y * cols, rows // Y

    half, core = rows_dev // CORES, lax.axis_index("col") % CORES

    def half_sketch(index):
        block = lax.dynamic_slice_in_dim(activations, index * half, half, 0)
        return jnp.dot(block, start_basis, preferred_element_type=jnp.float32)

    other = half_sketch(1 - core).astype(jnp.bfloat16)
    other = lax.ppermute(other, "col", [(c, c ^ 1) for c in range(cols)])
    mine = lax.optimization_barrier(half_sketch(core))
    partial = (mine + other.astype(jnp.float32)).astype(jnp.bfloat16)
    partial = partial.reshape(cols // CORES, -1, rank)
    parts = exchange(partial, "col", along_x)
    own = jnp.sum(parts.astype(jnp.float32), 0).astype(jnp.bfloat16)
    near, distance = own[None], CORES
    while distance < cols:
        near = jnp.concatenate([near, swap(near, distance)])
        distance *= 2
    far = swap(near, 1)

    gram = lax.dot_general(own, own, (((0,), (0,)), ((), ())), preferred_element_type=jnp.float32)
    gram = gram.reshape(plane_size, rank // plane_size, rank)
    gram = jnp.sum(exchange(gram, ("row", "col"), plane), 0)
    gram = jnp.sum(share(gram, depth, "row", along_z), 0)
    gram = share(gram, plane_size, ("row", "col"), plane).reshape(rank, rank)

    lines = rank // rows
    basis, projected = project(gram, near, far, activations, root_tokens, depth, lines)
    projected = projected.reshape(Y, rank // Y, -1)
    projected = jnp.sum(exchange(projected, "row", along_y).astype(jnp.float32), 0)
    projected = projected.astype(jnp.bfloat16).reshape(depth, lines, -1)
    projected = exchange(projected, "row", along_z).astype(jnp.float32)
    projected = jnp.sum(projected, 0)

    return (basis.T, projected)


def solution(mesh):
    return jax.shard_map(
        local,
        mesh=mesh,
        in_specs=(P("row", "col"), P("col", None)),
        out_specs=(P("row", "col"), P("row", "col")),
        check_vma=False,
    )
```
